256 devices in a mesh: blk: 16 (over z_hi, x), fsdp: 16 (over z_lo, y, core).
Axes of the slice: x: 4, y: 4, z: 8 (z_hi: 4, z_lo: 2; z = z_hi * 2 + z_lo), core: 2. Of those that a mesh axis runs over, the one named last changes fastest.
Arguments:
- inputs: bfloat16 [16, 6144, 1024], P('fsdp', 'blk'), may hold values from -6 to 6
- cotangent: bfloat16 [16, 6144, 1024], P('fsdp', 'blk'), may hold values from -6 to 6
- flags: int32 [16, 48, 16], P('fsdp', 'blk'), may hold values from 0 to 1, as said below
- w_qkv: bfloat16 [1024, 1536], P('fsdp'), may hold values from -0.1875 to 0.1875
- w_out: bfloat16 [512, 1024], P('fsdp'), may hold values from -0.25 to 0.25
- temper: float32 [8], replicated, may hold values from 0.5 to 8
Outputs:
- output: bfloat16 [16, 6144, 1024], P('fsdp', 'blk')
- grad_inputs: bfloat16 [16, 6144, 1024], P('fsdp', 'blk')
- grad_qkv: float32 [1024, 1536], P('fsdp')
- grad_out: float32 [512, 1024], P('fsdp')
The draws below stay inside these ranges and needn't reach their ends.
Inputs may be any that keep to these rules, and one draw needn't show every extreme that they name: `flags`: every token block may attend to the first anchor block of its own segment of 384 tokens.
All inputs are finite; a program needn't handle non-finite values.
Results may differ from the reference program's by a relative error of at most 0.015.
The reference program's roundings to bfloat16 on the way count: a program that leaves them out, or rounds other values in their place, can miss the bound.
Values may be sent and summed in bfloat16 or wider, within the bound.
No kernel may reach another device: no remote copies, remote signals or barrier semaphores. Data moves between devices by JAX's collectives and lax.ppermute only.
A program may use at most 128 MiB of HBM per device.

```python
import math
import jax
import jax.numpy as jnp
from jax import lax

D = 1024
HEADS = 8
HD = 64
BLOCK = 128
ANCH_DEV = 128
TOK_DEV = 384
INNER = 512
SEQ = 6144
MESHES = 16
ANCHORS = 2048
QBLOCKS = 48
ABLOCKS = 16
N_BLK = 16


def draw_flags(key, part):
    key = jax.random.fold_in(key, 11)
    level_key, roll_key = jax.random.split(key)
    per_dev = TOK_DEV // BLOCK
    segments = QBLOCKS // per_dev
    level = jax.random.randint(level_key, (MESHES, segments, 1, 1), 2, 15)
    roll = jax.random.randint(roll_key, (MESHES, segments, per_dev, ABLOCKS), 0, 16)
    column = jnp.arange(ABLOCKS)[None, None, None, :]
    owner = (jnp.arange(segments) * (ANCH_DEV // BLOCK))[None, :, None, None]
    keep = jnp.logical_or(roll < level, column == owner)
    return keep.astype(jnp.int32).reshape(MESHES, QBLOCKS, ABLOCKS)


def draw_temper(key, part):
    key = jax.random.fold_in(key, 5)
    spread = jax.random.uniform(key, (HEADS,), jnp.float32)
    return 0.5 * jnp.exp(spread * math.log(8.0))


def levels(key, shape, cuts, smallest, top_value):
    def one(position, parts):
        draws = jax.random.uniform(jax.random.fold_in(jax.random.fold_in(key, 6), position), (parts,), jnp.float32, smallest / len(cuts), top_value / len(cuts))
        return jnp.repeat(jnp.exp(draws), shape[position] // parts).reshape((-1,) + (1,) * (len(shape) - position - 1))

    level = one(*cuts[0])
    for cut in cuts[1:]:
        level = level * one(*cut)
    return level


def normal_values(own_key, dims, deviation, limit, cuts=(), kind=jnp.bfloat16):
    factor_of = levels(own_key, dims, cuts, -0.22, 0.18) if cuts else 1.0
    array = jax.random.normal(own_key, dims, jnp.float32) * deviation * factor_of
    return jnp.minimum(jnp.maximum(array, -limit), limit).astype(kind)


def setup_inputs(seed: int = 0) -> dict:
    streams_of = jax.random.split(jax.random.key(seed), 7)
    return {
        "inputs": normal_values(streams_of[0], (MESHES, SEQ, D), 1.0, 6.0, ((0, 16), (1, 16))),
        "cotangent": normal_values(streams_of[1], (MESHES, SEQ, D), 1.0, 6.0, ((0, 16), (1, 16))),
        "flags": draw_flags(jax.random.fold_in(streams_of[6], 71), 0),
        "w_qkv": normal_values(streams_of[3], (D, 3 * INNER), D ** -0.5, 0.1875, ((0, 16),)),
        "w_out": normal_values(streams_of[4], (INNER, D), INNER ** -0.5, 0.25, ((0, 16),)),
        "temper": draw_temper(jax.random.fold_in(streams_of[6], 71), 0),
    }


EPS = 1e-06

def row_scale(values):
    return jnp.sqrt(lax.optimization_barrier(jnp.mean(values * values, axis=-1, keepdims=True)) + EPS)

def head_norm(values):
    count = values.shape[0]
    shaped = values.reshape(count, HEADS, HD)
    scale = row_scale(shaped)
    return ((shaped / scale).reshape(count, HEADS * HD), scale)

def head_norm_back(grads, normed, scale):
    count = grads.shape[0]
    shaped = grads.reshape(count, HEADS, HD)
    unit = normed.reshape(count, HEADS, HD)
    inner = lax.optimization_barrier(jnp.mean(shaped * unit, axis=-1, keepdims=True))
    return ((shaped - unit * inner) / scale).reshape(count, HEADS * HD)

def segment_sum_rounded(left, right):
    count = left.shape[1]
    left_seg = left.reshape(N_BLK, TOK_DEV, count).astype(jnp.float32)
    right_seg = right.reshape(N_BLK, TOK_DEV, right.shape[1]).astype(jnp.float32)
    partial_sums = jnp.einsum('stc,std->scd', left_seg, right_seg).astype(jnp.bfloat16)
    partial_sums = lax.optimization_barrier(partial_sums)
    return lax.optimization_barrier(jnp.sum(partial_sums.astype(jnp.float32), axis=0))

def attend(queries, keys, values, upstream, allowed, temper):
    rows = queries.shape[0]
    count = keys.shape[0]
    width = queries.shape[1]

    def step(head, carry):
        out_acc, dq_acc, dk_acc, dv_acc = carry
        start = (jnp.asarray(head) * HD).astype(jnp.int32)
        q_head = lax.dynamic_slice_in_dim(queries, start, HD, 1)
        k_head = lax.dynamic_slice_in_dim(keys, start, HD, 1)
        v_head = lax.dynamic_slice_in_dim(values, start, HD, 1)
        u_head = lax.dynamic_slice_in_dim(upstream, start, HD, 1)
        factor = temper[head] / math.sqrt(HD)
        logits = jnp.dot(q_head, k_head.T, preferred_element_type=jnp.float32)
        scores = jnp.where(allowed, factor * logits, -jnp.inf)
        top = lax.optimization_barrier(jnp.max(scores, axis=1, keepdims=True))
        expo = jnp.exp(scores - top)
        probs = expo / lax.optimization_barrier(jnp.sum(expo, axis=1, keepdims=True))
        probs_b = probs.astype(jnp.bfloat16)
        out_head = jnp.dot(probs_b, v_head, preferred_element_type=jnp.float32)
        d_probs = jnp.dot(u_head, v_head.T, preferred_element_type=jnp.float32)
        delta = lax.optimization_barrier(jnp.sum(probs * d_probs, axis=1, keepdims=True))
        d_logit = (probs * (d_probs - delta) * factor).astype(jnp.bfloat16)
        dq_head = jnp.dot(d_logit, k_head, preferred_element_type=jnp.float32)
        dk_head = segment_sum_rounded(d_logit, q_head)
        dv_head = segment_sum_rounded(probs_b, u_head)
        out_acc = lax.dynamic_update_slice_in_dim(out_acc, out_head, start, 1)
        dq_acc = lax.dynamic_update_slice_in_dim(dq_acc, dq_head, start, 1)
        dk_acc = lax.dynamic_update_slice_in_dim(dk_acc, dk_head, start, 1)
        dv_acc = lax.dynamic_update_slice_in_dim(dv_acc, dv_head, start, 1)
        return (out_acc, dq_acc, dk_acc, dv_acc)
    init = (jnp.zeros((rows, width), jnp.float32), jnp.zeros((rows, width), jnp.float32), jnp.zeros((count, width), jnp.float32), jnp.zeros((count, width), jnp.float32))
    return lax.fori_loop(0, HEADS, step, init)

def one_mesh(tokens, upstream_in, flag_rows, w_qkv, w_out, temper):
    width = w_out.shape[0]
    xf = tokens.astype(jnp.float32)
    scale = row_scale(xf)
    normed = xf / scale
    xn = normed.astype(jnp.bfloat16)
    anchor_rows = xn.reshape(N_BLK, TOK_DEV, D)[:, :ANCH_DEV].reshape(ANCHORS, D)
    query = jnp.dot(xn, w_qkv[:, :width], preferred_element_type=jnp.float32)
    q_norm, q_scale = head_norm(query)
    q_bf = q_norm.astype(jnp.bfloat16)
    pair = jnp.dot(anchor_rows, w_qkv[:, width:], preferred_element_type=jnp.float32)
    k_norm, k_scale = head_norm(pair[:, :width])
    k_bf = k_norm.astype(jnp.bfloat16)
    v_bf = pair[:, width:].astype(jnp.bfloat16)
    upstream = jnp.dot(upstream_in, w_out.T, preferred_element_type=jnp.float32).astype(jnp.bfloat16)
    allowed = jnp.repeat(jnp.repeat(flag_rows > 0, BLOCK, axis=0), BLOCK, axis=1)
    out_acc, dq_acc, dk_acc, dv_acc = attend(q_bf, k_bf, v_bf, upstream, allowed, temper)
    attended = out_acc.astype(jnp.bfloat16)
    output = (xf + jnp.dot(attended, w_out, preferred_element_type=jnp.float32)).astype(jnp.bfloat16)
    dq_bf = head_norm_back(dq_acc, q_norm, q_scale).astype(jnp.bfloat16)
    dk_bf = head_norm_back(dk_acc, k_norm, k_scale).astype(jnp.bfloat16)
    dv_bf = dv_acc.astype(jnp.bfloat16)
    d_pair = jnp.concatenate([dk_bf, dv_bf], axis=1)
    d_normed = jnp.dot(dq_bf, w_qkv[:, :width].T, preferred_element_type=jnp.float32)
    anchor_part = jnp.dot(d_pair, w_qkv[:, width:].T, preferred_element_type=jnp.float32)
    d_normed = d_normed.reshape(N_BLK, TOK_DEV, D).at[:, :ANCH_DEV].add(anchor_part.reshape(N_BLK, ANCH_DEV, D)).reshape(SEQ, D)
    inner = lax.optimization_barrier(jnp.mean(d_normed * normed, axis=-1, keepdims=True))
    grad_in = (upstream_in.astype(jnp.float32) + (d_normed - normed * inner) / scale).astype(jnp.bfloat16)
    term_q = jnp.dot(xn.T, dq_bf, preferred_element_type=jnp.float32)
    term_kv = jnp.dot(anchor_rows.T, d_pair, preferred_element_type=jnp.float32)
    term_qkv = jnp.concatenate([term_q, term_kv], axis=1)
    term_out = jnp.dot(attended.T, upstream_in, preferred_element_type=jnp.float32)
    return (output, grad_in, term_qkv, term_out)

def reference(inputs, cotangent, flags, w_qkv, w_out, temper):

    def scan_step(carry, pieces):
        tokens, upstream_in, flag_rows = pieces
        output, grad_in, term_qkv, term_out = one_mesh(tokens, upstream_in, flag_rows, w_qkv, w_out, temper)
        return ((carry[0] + term_qkv, carry[1] + term_out), (output, grad_in))
    init = (jnp.zeros(w_qkv.shape, jnp.float32), jnp.zeros(w_out.shape, jnp.float32))
    sums, stacked = lax.scan(scan_step, init, (inputs, cotangent, flags))
    factor = 1.0 / math.sqrt(SEQ * MESHES)
    return (stacked[0], stacked[1], sums[0] * factor, sums[1] * factor)
```

```python
import math

import jax
import jax.numpy as jnp
from jax import lax
from jax.experimental import pallas as pl
from jax.experimental.pallas import tpu as pltpu
from jax.sharding import Mesh, PartitionSpec as P

HEADS = 8
HD = 64
BLOCK = 128
ANCH_DEV = 128
EPS = 1e-06
LOG2E = math.log2(math.e)
LN2 = math.log(2.0)
OFFSETS = (0, 3, 1, 2)
FSDP = ("zl", "y", "c")
BLK = ("zh", "x")
BF = jnp.bfloat16
F32 = jnp.float32
CHUNK = 256


def dot(a, b):
    return jnp.dot(a, b, preferred_element_type=F32)


def dot_nt(a, b):
    return lax.dot_general(a, b, (((1,), (1,)), ((), ())), preferred_element_type=F32)


def row_scale(values):
    return jnp.sqrt(jnp.mean(values * values, axis=-1, keepdims=True) + EPS)


def spread(left, right, lane):
    return jnp.where(lane < HD, left, right)


def pair_mean(values, lane):
    left = jnp.sum(jnp.where(lane < HD, values, 0.0), axis=-1, keepdims=True)
    right = jnp.sum(jnp.where(lane < HD, 0.0, values), axis=-1, keepdims=True)
    return spread(left, right, lane) * (1.0 / HD)


def attend_kernel(
    who_ref, temper_ref, xa_ref, xr_ref, u_ref, mask_ref, wq_ref, kaug_ref, vaug_ref,
    dk_in, dv_in, gq_in, back_ref, dk_ref, dv_ref, gq_ref, exp_ref,
):
    rows = xa_ref.shape[0] + xr_ref.shape[0]
    width = wq_ref.shape[1]
    anchors = kaug_ref.shape[0]
    pieces = anchors // CHUNK
    xf = jnp.concatenate([xa_ref[...], xr_ref[...]], axis=0).astype(F32)
    xn = (xf / row_scale(xf)).astype(BF)
    query = dot(xn, wq_ref[...])
    lane = lax.broadcasted_iota(jnp.int32, (rows, width), 1)
    q_inv = 1.0 / jnp.sqrt(pair_mean(query * query, lane) + EPS)
    q_norm = query * q_inv
    first = who_ref[0] * 2
    f_left = temper_ref[first] * (1.0 / math.sqrt(HD))
    f_right = temper_ref[first + 1] * (1.0 / math.sqrt(HD))
    factor = spread(f_left, f_right, lane)
    q_bf = (q_norm * (factor * LOG2E)).astype(BF)
    q_t = q_bf.astype(F32).T.astype(BF)
    up = u_ref[...].reshape(rows, width)
    up_t = up.astype(F32).T.astype(BF)
    start = who_ref[1] * (rows // BLOCK)
    mask = jnp.concatenate(
        [
            jnp.broadcast_to(mask_ref[pl.ds(start + i, 1), :], (BLOCK, width))
            for i in range(rows // BLOCK)
        ],
        axis=0,
    ).astype(BF)
    out = jnp.zeros((rows, width), F32)
    dqn = jnp.zeros((rows, width), F32)
    for head in range(2):
        sel = (lane < HD) if head == 0 else (lane >= HD)
        span = slice(head * HD, head * HD + HD)
        q_aug = jnp.concatenate([jnp.where(sel, q_bf, 0), mask], axis=1)
        acc = jnp.zeros((rows, 2 * width), F32)
        for c in range(pieces):
            part = slice(c * CHUNK, c * CHUNK + CHUNK)
            expo = jnp.exp2(dot_nt(q_aug, kaug_ref[part, :]))
            exp_ref[:, part] = expo.astype(BF)
            acc = acc + dot(exp_ref[:, part], vaug_ref[part, :])
        inv = 1.0 / acc[:, width : width + 1]
        out_h = acc[:, :width] * inv
        out = jnp.where(sel, out_h, out)
        u_h = jnp.where(sel, up, 0)
        delta = -jnp.sum(out_h * u_h.astype(F32), axis=1, keepdims=True)
        d_hi = delta.astype(BF)
        d_lo = (delta - d_hi.astype(F32)).astype(BF)
        tail = jnp.where(lane == 0, d_hi.astype(F32), jnp.where(lane == 1, d_lo.astype(F32), 0.0))
        u_aug = jnp.concatenate([u_h, tail.astype(BF)], axis=1)
        dq_h = jnp.zeros((rows, width), F32)
        for c in range(pieces):
            part = slice(c * CHUNK, c * CHUNK + CHUNK)
            dp = dot_nt(u_aug, vaug_ref[part, :])
            prob = exp_ref[:, part].astype(F32) * inv
            prob_b = prob.astype(BF)
            dz = (prob * dp).astype(BF)
            dq_h = dq_h + dot(dz, kaug_ref[part, :width])
            dk_ref[span, part] = dk_in[span, part] + dot(q_t[span, :], dz)
            dv_ref[span, part] = dv_in[span, part] + dot(up_t[span, :], prob_b)
        dqn = jnp.where(sel, dq_h, dqn)
    dqn = dqn * factor
    dqb = ((dqn - q_norm * pair_mean(dqn * q_norm, lane)) * q_inv).astype(BF)
    back_ref[:, :width] = out.astype(BF)
    back_ref[:, width:] = dqb
    gq_ref[...] = gq_in[...] + dot(dqb.astype(F32).T.astype(BF), xn)


def attend(who, temper, xa, xr, up, mask, wq, kaug, vaug, dk, dv, gq):
    rows = xa.shape[0] + xr.shape[0]
    width = wq.shape[1]
    anchors = kaug.shape[0]
    vmem = pl.BlockSpec(memory_space=pltpu.VMEM)
    smem = pl.BlockSpec(memory_space=pltpu.SMEM)
    return pl.pallas_call(
        attend_kernel,
        out_shape=(
            jax.ShapeDtypeStruct((rows, 2 * width), BF),
            jax.ShapeDtypeStruct(dk.shape, F32),
            jax.ShapeDtypeStruct(dv.shape, F32),
            jax.ShapeDtypeStruct(gq.shape, F32),
        ),
        in_specs=[smem, smem] + [vmem] * 10,
        out_specs=(vmem, vmem, vmem, vmem),
        scratch_shapes=[pltpu.VMEM((rows, anchors), BF)],
        compiler_params=pltpu.CompilerParams(vmem_limit_bytes=56 * 1024 * 1024),
        cost_estimate=pl.CostEstimate(
            flops=14 * rows * anchors * width * 4,
            bytes_accessed=8 * 1024 * 1024,
            transcendentals=2 * rows * anchors,
        ),
    )(who, temper, xa, xr, up, mask, wq, kaug, vaug, dk, dv, gq)


def shift(offset):
    return [(i, (i - offset) % 4) for i in range(4)]


def unshift(offset):
    return [(i, (i + offset) % 4) for i in range(4)]


def fan(values, axis, count):
    spread_out = jnp.broadcast_to(values[None], (count,) + values.shape)
    return lax.all_to_all(spread_out, axis, 0, 0)


def columns(values, index, width):
    return lax.dynamic_slice_in_dim(values, index * width, width, 1)


def on_device(inputs, cotangent, flags, w_qkv, w_out, temper):
    x_at = lax.axis_index("x")
    z_at = lax.axis_index("zh")
    tokens = inputs[0]
    upstream_in = cotangent[0]
    inner = w_qkv.shape[1] // 3
    wide = inner // 4
    fsdp_count = lax.axis_size(FSDP)
    first = tokens[:ANCH_DEV]
    rest = tokens[ANCH_DEV:]
    xa_parts = [first] + [lax.ppermute(first, "x", shift(o)) for o in OFFSETS[1:]]
    chosen = jnp.concatenate([columns(w_qkv, j * 4 + x_at, wide) for j in range(3)], axis=1)
    chosen = fan(chosen, FSDP, fsdp_count).reshape(-1, 3 * wide)
    xr_parts = [rest] + [lax.ppermute(rest, "x", shift(o)) for o in OFFSETS[1:]]
    weights = lax.all_gather(w_qkv, FSDP, axis=0, tiled=True)
    projection = lax.all_gather(w_out, FSDP, axis=0, tiled=True)
    flag_rows = lax.all_gather(flags[0], "x", axis=0, tiled=True)

    xa_f = jnp.concatenate(xa_parts, axis=0).astype(F32)
    xa_n = (xa_f / row_scale(xa_f)).astype(BF)
    pair = dot(xa_n, chosen[:, wide:])
    lane = lax.broadcasted_iota(jnp.int32, (1, wide), 1)
    key = pair[:, :wide]
    k_inv = 1.0 / jnp.sqrt(pair_mean(key * key, lane) + EPS)
    k_norm = key * k_inv
    kv = jnp.concatenate([k_norm, pair[:, wide:]], axis=1).astype(BF)
    kv_all = fan(kv, "zh", 4).reshape(-1, 2 * wide)
    anchors = kv_all.shape[0]
    place = lax.broadcasted_iota(jnp.int32, (anchors, wide), 0) // ANCH_DEV
    turn = jnp.where(place % 4 == 0, 0, jnp.where(place % 4 == 1, 3, place % 4 - 1))
    segment = place // 4 * 4 + (x_at + turn) % 4
    column = lax.broadcasted_iota(jnp.int32, (anchors, wide), 1)
    kaug = jnp.concatenate([kv_all[:, :wide], (segment == column).astype(BF)], axis=1)
    vaug = jnp.concatenate([kv_all[:, wide:], (column < 2).astype(BF)], axis=1)
    mask = jnp.where(flag_rows > 0, 0.0, -1024.0).astype(F32)
    mask = jnp.pad(mask, ((0, 4), (0, wide - mask.shape[1])))

    upstream = dot_nt(upstream_in, projection).astype(BF)
    rows = tokens.shape[0]
    up_all = lax.all_to_all(upstream.reshape(rows, 4, wide), "x", 1, 0)

    dk = jnp.zeros((wide, anchors), F32)
    dv = jnp.zeros((wide, anchors), F32)
    gq = jnp.zeros((wide, tokens.shape[1]), F32)
    sent = []
    for r, o in enumerate(OFFSETS):
        at = (x_at + o) % 4
        up = lax.dynamic_index_in_dim(up_all, at, 0, keepdims=False)
        who = jnp.stack([x_at, at])
        back, dk, dv, gq = attend(
            who, temper, xa_parts[r], xr_parts[r], up, mask, chosen[:, :wide],
            kaug, vaug, dk, dv, gq,
        )
        sent.append(back if o == 0 else lax.ppermute(back, "x", unshift(o)))

    both = jnp.concatenate([dk * LN2, dv], axis=0).reshape(2 * wide, 4, anchors // 4)
    both = lax.all_to_all(both.astype(BF), "zh", 1, 0)
    both = jnp.sum(both.astype(F32), axis=0).T
    dkn = both[:, :wide]
    dkb = (dkn - k_norm * pair_mean(dkn * k_norm, lane)) * k_inv
    dkv = jnp.concatenate([dkb, both[:, wide:]], axis=1).astype(BF)
    dkv_parts = [dkv[:ANCH_DEV]] + [
        lax.ppermute(dkv[i * ANCH_DEV : (i + 1) * ANCH_DEV], "x", unshift(OFFSETS[i]))
        for i in (1, 2, 3)
    ]
    term_kv = lax.dot_general(xa_n, dkv, (((0,), (0,)), ((), ())), preferred_element_type=F32)

    order = [(x_at - o) % 4 for o in OFFSETS]
    attended = jnp.concatenate([part[:, :wide] for part in sent], axis=1)
    dqb = jnp.concatenate([part[:, wide:] for part in sent], axis=1)
    w_back = jnp.concatenate(
        [lax.dynamic_slice_in_dim(projection, at * wide, wide, 0) for at in order], axis=0
    )
    w_q = jnp.concatenate([columns(weights, at, wide) for at in order], axis=1)
    w_kv = jnp.concatenate(
        [columns(weights, 4 * j + at, wide) for at in order for j in (1, 2)], axis=1
    )
    xf = tokens.astype(F32)
    scale = row_scale(xf)
    normed = xf / scale
    output = (xf + dot(attended, w_back)).astype(BF)
    d_normed = dot_nt(dqb, w_q)
    d_normed = d_normed.at[:ANCH_DEV].add(dot_nt(jnp.concatenate(dkv_parts, axis=1), w_kv))
    mean = jnp.mean(d_normed * normed, axis=-1, keepdims=True)
    grad_in = (upstream_in.astype(F32) + (d_normed - normed * mean) / scale).astype(BF)

    count = rows * lax.axis_size(BLK) * fsdp_count
    norm = 1.0 / math.sqrt(count)
    term_out = lax.dot_general(
        attended, upstream_in, (((0,), (0,)), ((), ())), preferred_element_type=F32
    )
    slots = [(x_at - a) % 4 for a in range(4)]
    where_at = [jnp.where(s == 3, 1, jnp.where(s == 1, 2, jnp.where(s == 2, 3, 0))) for s in slots]
    term_out = jnp.concatenate(
        [lax.dynamic_slice_in_dim(term_out, at * wide, wide, 0) for at in where_at], axis=0
    )
    term_out = (term_out * norm).astype(BF).reshape(fsdp_count, -1, term_out.shape[1])
    term_out = lax.all_to_all(term_out, FSDP, 0, 0)
    term_out = jnp.sum(term_out.astype(F32), axis=0).astype(BF)
    term_qkv = jnp.concatenate([gq.T, term_kv], axis=1) * norm
    term_qkv = term_qkv.astype(BF).reshape(fsdp_count, -1, 3 * wide)
    term_qkv = lax.all_to_all(term_qkv, FSDP, 0, 0)
    term_qkv = jnp.sum(term_qkv.astype(F32), axis=0).astype(BF)

    out_z = jnp.sum(fan(term_out, "zh", 4).astype(F32), axis=0).astype(BF)
    grad_out = jnp.sum(fan(out_z, "x", 4).astype(F32), axis=0)
    qkv_z = jnp.sum(fan(term_qkv, "zh", 4).astype(F32), axis=0).astype(BF)
    qkv_x = fan(qkv_z, "x", 4).astype(F32)
    share = qkv_x.shape[1]
    grad_qkv = qkv_x.reshape(4, share, 3, wide).transpose(1, 2, 0, 3).reshape(share, 3 * inner)
    return (output[None], grad_in[None], grad_qkv, grad_out)


def solution(mesh):
    split = Mesh(mesh.devices.reshape(4, 4, 2, 4, 2), BLK + FSDP)
    placed = (
        P(FSDP, BLK, None),
        P(FSDP, BLK, None),
        P(FSDP, BLK, None),
        P(FSDP, None),
        P(FSDP, None),
        P(),
    )
    return jax.shard_map(
        on_device,
        mesh=split,
        in_specs=placed,
        out_specs=(
            P(FSDP, BLK, None),
            P(FSDP, BLK, None),
            P(FSDP, None),
            P(FSDP, None),
        ),
        check_vma=False,
    )
```

```python
import functools
import math

import jax
import jax.numpy as jnp
from jax import lax
from jax.experimental import pallas as pl
from jax.experimental.pallas import tpu as pltpu
from jax.sharding import Mesh, PartitionSpec as P

HEADS = 8
HD = 64
BLOCK = 128
ANCH_DEV = 128
EPS = 1e-06
FLAG_ROWS = 16
LOG2E = math.log2(math.e)
LN2 = math.log(2.0)
OFFSETS = (0, 3, 1, 2)
FSDP = ("zl", "y", "c")
BLK = ("zh", "x")
BF = jnp.bfloat16
F32 = jnp.float32
CHUNK = 256


def dot(a, b):
    return jnp.dot(a, b, preferred_element_type=F32)


def dot_nt(a, b):
    return lax.dot_general(a, b, (((1,), (1,)), ((), ())), preferred_element_type=F32)


def row_scale(values):
    return jnp.sqrt(jnp.mean(values * values, axis=-1, keepdims=True) + EPS)


def spread(left, right, lane):
    return jnp.where(lane < HD, left, right)


def pair_mean(values, lane):
    left = jnp.sum(jnp.where(lane < HD, values, 0.0), axis=-1, keepdims=True)
    right = jnp.sum(jnp.where(lane < HD, 0.0, values), axis=-1, keepdims=True)
    return spread(left, right, lane) * (1.0 / HD)


def attend_kernel(norm, *refs):
    temper_ref, *refs = refs
    xa_refs, xr_refs, refs = refs[:4], refs[4:8], refs[8:]
    up_refs, refs = refs[:4], refs[4:]
    wq_ref, kaug_ref, vaug_ref, *refs = refs
    back_refs, both_ref, refs = refs[:4], refs[4], refs[5:]
    gq_out, xn_ref, u_ref, mask_ref, back_all, dk_ref, dv_ref, gq_ref, exp_ref = refs
    x_at = lax.axis_index("x")
    rows = xn_ref.shape[1]
    width = wq_ref.shape[1]
    pieces = dk_ref.shape[0]
    for r in range(4):
        u_ref[r] = up_refs[r][...]
        for lo, ref in ((0, xa_refs[r]), (ANCH_DEV, xr_refs[r])):
            for start in range(0, rows - ANCH_DEV if lo else ANCH_DEV, BLOCK):
                xf = ref[start : start + BLOCK, :].astype(F32)
                xn_ref[r, lo + start : lo + start + BLOCK, :] = (xf / row_scale(xf)).astype(BF)
        flag_rows = xa_refs[r][ANCH_DEV : ANCH_DEV + FLAG_ROWS, :width].astype(F32)
        mask_ref[r] = jnp.where(flag_rows > 0.0, 0.0, -1024.0)
    dk_ref[...] = jnp.zeros_like(dk_ref)
    dv_ref[...] = jnp.zeros_like(dv_ref)
    gq_ref[...] = jnp.zeros_like(gq_ref)
    lane = lax.broadcasted_iota(jnp.int32, (rows, width), 1)
    first = x_at * 2
    f_left = temper_ref[first] * (1.0 / math.sqrt(HD))
    f_right = temper_ref[first + 1] * (1.0 / math.sqrt(HD))
    factor = spread(f_left, f_right, lane)

    def chunk(i, carry):
        xn = xn_ref[i]
        query = dot(xn, wq_ref[...])
        q_inv = 1.0 / jnp.sqrt(pair_mean(query * query, lane) + EPS)
        q_norm = query * q_inv
        q_bf = (q_norm * (factor * LOG2E)).astype(BF)
        q_t = q_bf.astype(F32).T.astype(BF)
        up = u_ref[i]
        up_t = up.astype(F32).T.astype(BF)
        mask_rows = mask_ref[i]
        mask = jnp.concatenate(
            [
                jnp.broadcast_to(mask_rows[j : j + 1, :], (BLOCK, width))
                for j in range(rows // BLOCK)
            ],
            axis=0,
        ).astype(BF)
        out = jnp.zeros((rows, width), F32)
        dqn = jnp.zeros((rows, width), F32)
        for head in range(2):
            sel = (lane < HD) if head == 0 else (lane >= HD)
            span = slice(head * HD, head * HD + HD)
            q_aug = jnp.concatenate([jnp.where(sel, q_bf, 0), mask], axis=1)
            acc = jnp.zeros((rows, 2 * width), F32)
            for c in range(pieces):
                part = slice(c * CHUNK, c * CHUNK + CHUNK)
                expo = jnp.exp2(dot_nt(q_aug, kaug_ref[part, :])).astype(BF)
                exp_ref[head, c] = expo
                acc = acc + dot(expo, vaug_ref[part, :])
            inv = 1.0 / acc[:, width : width + 1]
            out_h = acc[:, :width] * inv
            out = jnp.where(sel, out_h, out)
            u_h = jnp.where(sel, up, 0)
            delta = -jnp.sum(out_h * u_h.astype(F32), axis=1, keepdims=True)
            d_hi = delta.astype(BF).astype(F32)
            tail = jnp.where(lane == 0, d_hi, jnp.where(lane == 1, delta - d_hi, 0.0))
            u_aug = jnp.concatenate([u_h, tail.astype(BF)], axis=1)
            dq_h = jnp.zeros((rows, width), F32)
            for c in range(pieces):
                part = slice(c * CHUNK, c * CHUNK + CHUNK)
                dp = dot_nt(u_aug, vaug_ref[part, :])
                prob = exp_ref[head, c].astype(F32) * inv
                dz = (prob * dp).astype(BF)
                dq_h = dq_h + dot(dz, kaug_ref[part, :width])
                dk_ref[c, span, :] = dk_ref[c, span, :] + dot(q_t[span, :], dz)
                dv_ref[c, span, :] = dv_ref[c, span, :] + dot(up_t[span, :], prob.astype(BF))
            dqn = jnp.where(sel, dq_h, dqn)
        dqn = dqn * factor
        dqb = ((dqn - q_norm * pair_mean(dqn * q_norm, lane)) * q_inv).astype(BF)
        back_all[i, :, :width] = out.astype(BF)
        back_all[i, :, width:] = dqb
        gq_ref[...] = gq_ref[...] + dot(dqb.astype(F32).T.astype(BF), xn)
        return carry

    lax.fori_loop(0, 4, chunk, 0)
    per = pieces // 4
    for r in range(4):
        back_refs[r][...] = back_all[r]
        for c in range(per):
            part = slice(c * CHUNK, c * CHUNK + CHUNK)
            both_ref[r, :width, part] = (dk_ref[r * per + c] * LN2).astype(BF)
            both_ref[r, width:, part] = dv_ref[r * per + c].astype(BF)
    gq_out[...] = (gq_ref[...] * norm).T.astype(BF)


def attend(norm, temper, xa_parts, xr_parts, up_parts, wq, kaug, vaug):
    rows = ANCH_DEV + xr_parts[0].shape[0]
    depth, width = wq.shape
    anchors = kaug.shape[0]
    vmem = pl.BlockSpec(memory_space=pltpu.VMEM)
    smem = pl.BlockSpec(memory_space=pltpu.SMEM)
    back = jax.ShapeDtypeStruct((rows, 2 * width), BF)
    both = jax.ShapeDtypeStruct((4, 2 * width, anchors // 4), BF)
    pieces = anchors // CHUNK
    outs = pl.pallas_call(
        functools.partial(attend_kernel, norm),
        out_shape=(back,) * 4 + (both,) + (jax.ShapeDtypeStruct((depth, width), BF),),
        in_specs=[smem] + [vmem] * 15,
        out_specs=(vmem,) * 6,
        scratch_shapes=[
            pltpu.VMEM((4, rows, depth), BF),
            pltpu.VMEM((4, rows, width), BF),
            pltpu.VMEM((4, FLAG_ROWS, width), F32),
            pltpu.VMEM((4, rows, 2 * width), BF),
            pltpu.VMEM((pieces, width, CHUNK), F32),
            pltpu.VMEM((pieces, width, CHUNK), F32),
            pltpu.VMEM((width, depth), F32),
            pltpu.VMEM((2, pieces, rows, CHUNK), BF),
        ],
        compiler_params=pltpu.CompilerParams(vmem_limit_bytes=56 * 1024 * 1024),
        cost_estimate=pl.CostEstimate(
            flops=14 * 4 * rows * anchors * width * 4,
            bytes_accessed=8 * 1024 * 1024,
            transcendentals=2 * 4 * rows * anchors,
        ),
    )(temper, *xa_parts, *xr_parts, *up_parts, wq, kaug, vaug)
    return outs[:4], outs[4], outs[5]


def tie(*values):
    return lax.optimization_barrier(values)


def shift(offset):
    return [(i, (i - offset) % 4) for i in range(4)]


def unshift(offset):
    return [(i, (i + offset) % 4) for i in range(4)]


def fan(values, axis, count):
    spread_out = jnp.broadcast_to(values[None], (count,) + values.shape)
    return lax.all_to_all(spread_out, axis, 0, 0)


def placed_at(parts, index):
    out = []
    for a in range(4):
        step = (index - a) % 4
        pick = parts[0]
        for r in (1, 2, 3):
            pick = jnp.where(step == OFFSETS[r], parts[r], pick)
        out.append(pick)
    return out


def columns(values, index, width):
    return lax.dynamic_slice_in_dim(values, index * width, width, 1)


def on_device(inputs, cotangent, flags, w_qkv, w_out, temper):
    x_at = lax.axis_index("x")
    tokens = inputs[0]
    upstream_in = cotangent[0]
    inner = w_qkv.shape[1] // 3
    wide = inner // 4
    fsdp_count = lax.axis_size(FSDP)
    rows = tokens.shape[0]
    flag_rows = jnp.pad(
        flags[0].astype(BF),
        ((0, FLAG_ROWS - flags.shape[1]), (0, tokens.shape[1] - flags.shape[2])),
    )
    first = jnp.concatenate([tokens[:ANCH_DEV], flag_rows], axis=0)
    rest = tokens[ANCH_DEV:]
    xa_parts = [first] + [lax.ppermute(first, "x", shift(o)) for o in OFFSETS[1:]]
    width = tokens.shape[1]
    chosen = jnp.concatenate([columns(w_qkv, j * 4 + x_at, wide) for j in range(3)], axis=1)
    chosen = jnp.concatenate([w_out, chosen.reshape(-1, width)], axis=0)
    chosen = fan(chosen, FSDP, fsdp_count)
    lines = w_out.shape[0]
    projection = chosen[:, :lines].reshape(inner, width)
    chosen = chosen[:, lines:].reshape(-1, 3 * wide)

    *xa_parts, rest = tie(*xa_parts, rest)
    xr_parts = [rest] + [lax.ppermute(rest, "x", shift(o)) for o in OFFSETS[1:]]

    xa_f = jnp.concatenate([part[:ANCH_DEV] for part in xa_parts], axis=0).astype(F32)
    xa_n = (xa_f / row_scale(xa_f)).astype(BF)
    pair = dot(xa_n, chosen[:, wide:])
    lane = lax.broadcasted_iota(jnp.int32, (1, wide), 1)
    key = pair[:, :wide]
    k_inv = 1.0 / jnp.sqrt(pair_mean(key * key, lane) + EPS)
    k_norm = key * k_inv
    kv = jnp.concatenate([k_norm, pair[:, wide:]], axis=1).astype(BF)
    kv, xr_parts[1], xr_parts[2], ahead = tie(kv, xr_parts[1], xr_parts[2], upstream_in)
    kv_all = fan(kv, "zh", 4)
    upstream = dot_nt(ahead, projection).astype(BF)
    up_parts = [columns(upstream, (x_at - o) % 4, wide) for o in OFFSETS]
    up_parts = [up_parts[0]] + [
        lax.ppermute(up_parts[i], "x", shift(OFFSETS[i])) for i in (1, 2, 3)
    ]
    kv_all, *up_parts = tie(kv_all, *up_parts)
    kv_all = kv_all.reshape(-1, 2 * wide)
    anchors = kv_all.shape[0]
    place = lax.broadcasted_iota(jnp.int32, (anchors, wide), 0) // ANCH_DEV

    def turn(i):
        return jnp.where(i == 0, 0, jnp.where(i == 1, 3, i - 1))

    segment = place // 4 * 4 + (x_at + turn(place % 4)) % 4
    column = lax.broadcasted_iota(jnp.int32, (anchors, wide), 1)
    kaug = jnp.concatenate([kv_all[:, :wide], (segment == column).astype(BF)], axis=1)
    vaug = jnp.concatenate([kv_all[:, wide:], (column < 2).astype(BF)], axis=1)
    kaug, w_mine = tie(kaug, w_qkv)
    weights = lax.all_gather(w_mine, FSDP, axis=0, tiled=True)

    count = rows * lax.axis_size(BLK) * fsdp_count
    norm = 1.0 / math.sqrt(count)
    backs, both, term_q = attend(
        norm, temper, xa_parts, xr_parts, up_parts, chosen[:, :wide], kaug, vaug
    )

    both = lax.all_to_all(both, "zh", 0, 0)
    sent = [backs[0]] + [lax.ppermute(backs[i], "x", unshift(OFFSETS[i])) for i in (1, 2, 3)]
    sent = placed_at(sent, x_at)
    attended = jnp.concatenate([part[:, :wide] for part in sent], axis=1)
    dqb = jnp.concatenate([part[:, wide:] for part in sent], axis=1)
    term_out = lax.dot_general(
        attended, upstream_in, (((0,), (0,)), ((), ())), preferred_element_type=F32
    )
    term_out = (term_out * norm).reshape(fsdp_count, 4, -1, width)
    pieces = [
        lax.dynamic_index_in_dim(term_out, (x_at + o) % 4, 1, keepdims=False) for o in OFFSETS
    ]
    term_out = pieces[0]
    for i in (1, 2, 3):
        term_out += lax.ppermute(pieces[i].astype(BF), "x", unshift(OFFSETS[i])).astype(F32)
    term_out = term_out.astype(BF)
    both, term_out = tie(both, term_out)

    total = jnp.sum(both.astype(F32), axis=0)
    total = total.T
    dkn = total[:, :wide]
    dkb = (dkn - k_norm * pair_mean(dkn * k_norm, lane)) * k_inv
    dkv = jnp.concatenate([dkb, total[:, wide:]], axis=1).astype(BF)
    term_kv = lax.dot_general(xa_n, dkv, (((0,), (0,)), ((), ())), preferred_element_type=F32)
    term_kv = (term_kv * norm).astype(BF).reshape(fsdp_count, -1, width)
    late = [term_out, term_q.reshape(fsdp_count, -1, width), term_kv]
    late = lax.all_to_all(jnp.concatenate(late, axis=1), FSDP, 0, 0)
    dkv_parts = [dkv[:ANCH_DEV]] + [
        lax.ppermute(dkv[i * ANCH_DEV : (i + 1) * ANCH_DEV], "x", unshift(OFFSETS[i]))
        for i in (1, 2, 3)
    ]
    dkv_parts = placed_at(dkv_parts, x_at)
    xf = tokens.astype(F32)
    scale = row_scale(xf)
    normed = xf / scale
    output = (xf + dot(attended, projection)).astype(BF)
    d_normed = dot_nt(dqb, weights[:, :inner])
    d_pair = jnp.concatenate(
        [part[:, :wide] for part in dkv_parts] + [part[:, wide:] for part in dkv_parts], axis=1
    )
    d_normed = d_normed.at[:ANCH_DEV].add(dot_nt(d_pair, weights[:, inner:]))
    mean = jnp.mean(d_normed * normed, axis=-1, keepdims=True)
    grad_in = (upstream_in.astype(F32) + (d_normed - normed * mean) / scale).astype(BF)

    late, grad_in, output = tie(late, grad_in, output)
    late = jnp.sum(late.astype(F32), axis=0).astype(BF)
    late_parts = [late] + [lax.ppermute(late, "zh", shift(o)) for o in OFFSETS[1:]]
    late = sum(part.astype(F32) for part in late_parts).astype(BF)
    late_parts = [late] + [lax.ppermute(late, "x", unshift(o)) for o in OFFSETS[1:]]
    late_parts = placed_at([part.astype(F32) for part in late_parts], x_at)
    lines = lines // 4
    grad_out = jnp.concatenate([part[:lines] for part in late_parts], axis=0)
    late_parts = [part[lines:] for part in late_parts]
    share = w_qkv.shape[0]
    deep = wide * share // width
    part_q = [part[:deep].reshape(share, wide) for part in late_parts]
    part_kv = [part[deep:].reshape(share, 2 * wide) for part in late_parts]
    grad_qkv = jnp.concatenate(
        part_q + [part[:, :wide] for part in part_kv] + [part[:, wide:] for part in part_kv],
        axis=1,
    )
    return (output[None], grad_in[None], grad_qkv, grad_out)


def solution(mesh):
    split = Mesh(mesh.devices.reshape(4, 4, 2, 4, 2), BLK + FSDP)
    placed = (
        P(FSDP, BLK, None),
        P(FSDP, BLK, None),
        P(FSDP, BLK, None),
        P(FSDP, None),
        P(FSDP, None),
        P(),
    )
    return jax.shard_map(
        on_device,
        mesh=split,
        in_specs=placed,
        out_specs=(
            P(FSDP, BLK, None),
            P(FSDP, BLK, None),
            P(FSDP, None),
            P(FSDP, None),
        ),
        check_vma=False,
    )
```

```python
import functools
import math

import jax
import jax.numpy as jnp
from jax import lax
from jax.experimental import pallas as pl
from jax.experimental.pallas import tpu as pltpu
from jax.sharding import Mesh, PartitionSpec as P

HEADS = 8
HD = 64
BLOCK = 128
ANCH_DEV = 128
EPS = 1e-06
FLAG_ROWS = 16
LOG2E = math.log2(math.e)
LN2 = math.log(2.0)
OFFSETS = (0, 3, 1, 2)
FSDP = ("zl", "y", "c")
BLK = ("zh", "x")
BF = jnp.bfloat16
F32 = jnp.float32
CHUNK = 256


def dot(a, b):
    return jnp.dot(a, b, preferred_element_type=F32)


def dot_nt(a, b):
    return lax.dot_general(a, b, (((1,), (1,)), ((), ())), preferred_element_type=F32)


def row_scale(values):
    return jnp.sqrt(jnp.mean(values * values, axis=-1, keepdims=True) + EPS)


def spread(left, right, lane):
    return jnp.where(lane < HD, left, right)


def pair_mean(values, lane):
    left = jnp.sum(jnp.where(lane < HD, values, 0.0), axis=-1, keepdims=True)
    right = jnp.sum(jnp.where(lane < HD, 0.0, values), axis=-1, keepdims=True)
    return spread(left, right, lane) * (1.0 / HD)


def attend_kernel(norm, *refs):
    temper_ref, *refs = refs
    xa_refs, xr_refs, refs = refs[:4], refs[4:8], refs[8:]
    up_refs, refs = refs[:4], refs[4:]
    wq_ref, kaug_ref, vaug_ref, *refs = refs
    back_refs, both_ref, refs = refs[:4], refs[4], refs[5:]
    gq_out, xn_ref, u_ref, mask_ref, back_all, dk_ref, dv_ref, gq_ref, exp_ref = refs
    x_at = lax.axis_index("x")
    z_at = lax.axis_index("zh")
    rows = xn_ref.shape[1]
    width = wq_ref.shape[1]
    pieces = dk_ref.shape[0]
    for r in range(4):
        u_ref[r] = up_refs[r][...]
        for lo, ref in ((0, xa_refs[r]), (ANCH_DEV, xr_refs[r])):
            for start in range(0, rows - ANCH_DEV if lo else ANCH_DEV, BLOCK):
                xf = ref[start : start + BLOCK, :].astype(F32)
                xn_ref[r, lo + start : lo + start + BLOCK, :] = (xf / row_scale(xf)).astype(BF)
        flag_rows = xa_refs[r][ANCH_DEV : ANCH_DEV + FLAG_ROWS, :width].astype(F32)
        mask_ref[r] = jnp.where(flag_rows > 0.0, 0.0, -1024.0)
    dk_ref[...] = jnp.zeros_like(dk_ref)
    dv_ref[...] = jnp.zeros_like(dv_ref)
    gq_ref[...] = jnp.zeros_like(gq_ref)
    lane = lax.broadcasted_iota(jnp.int32, (rows, width), 1)
    first = x_at * 2
    f_left = temper_ref[first] * (1.0 / math.sqrt(HD))
    f_right = temper_ref[first + 1] * (1.0 / math.sqrt(HD))
    factor = spread(f_left, f_right, lane)

    def chunk(i, carry):
        xn = xn_ref[i]
        query = dot(xn, wq_ref[...])
        q_inv = 1.0 / jnp.sqrt(pair_mean(query * query, lane) + EPS)
        q_norm = query * q_inv
        q_bf = (q_norm * (factor * LOG2E)).astype(BF)
        q_t = q_bf.astype(F32).T.astype(BF)
        up = u_ref[i]
        up_t = up.astype(F32).T.astype(BF)
        mask_rows = mask_ref[i]
        mask = jnp.concatenate(
            [
                jnp.broadcast_to(mask_rows[j : j + 1, :], (BLOCK, width))
                for j in range(rows // BLOCK)
            ],
            axis=0,
        ).astype(BF)
        out = jnp.zeros((rows, width), F32)
        dqn = jnp.zeros((rows, width), F32)
        for head in range(2):
            sel = (lane < HD) if head == 0 else (lane >= HD)
            span = slice(head * HD, head * HD + HD)
            q_aug = jnp.concatenate([jnp.where(sel, q_bf, 0), mask], axis=1)
            acc = jnp.zeros((rows, 2 * width), F32)
            for c in range(pieces):
                part = slice(c * CHUNK, c * CHUNK + CHUNK)
                expo = jnp.exp2(dot_nt(q_aug, kaug_ref[part, :])).astype(BF)
                exp_ref[head, c] = expo
                acc = acc + dot(expo, vaug_ref[part, :])
            inv = 1.0 / acc[:, width : width + 1]
            out_h = acc[:, :width] * inv
            out = jnp.where(sel, out_h, out)
            u_h = jnp.where(sel, up, 0)
            delta = -jnp.sum(out_h * u_h.astype(F32), axis=1, keepdims=True)
            d_hi = delta.astype(BF).astype(F32)
            tail = jnp.where(lane == 0, d_hi, jnp.where(lane == 1, delta - d_hi, 0.0))
            u_aug = jnp.concatenate([u_h, tail.astype(BF)], axis=1)
            dq_h = jnp.zeros((rows, width), F32)
            for c in range(pieces):
                part = slice(c * CHUNK, c * CHUNK + CHUNK)
                dp = dot_nt(u_aug, vaug_ref[part, :])
                prob = exp_ref[head, c].astype(F32) * inv
                dz = (prob * dp).astype(BF)
                dq_h = dq_h + dot(dz, kaug_ref[part, :width])
                dk_ref[c, span, :] = dk_ref[c, span, :] + dot(q_t[span, :], dz)
                dv_ref[c, span, :] = dv_ref[c, span, :] + dot(up_t[span, :], prob.astype(BF))
            dqn = jnp.where(sel, dq_h, dqn)
        dqn = dqn * factor
        dqb = ((dqn - q_norm * pair_mean(dqn * q_norm, lane)) * q_inv).astype(BF)
        back_all[i, :, :width] = out.astype(BF)
        back_all[i, :, width:] = dqb
        gq_ref[...] = gq_ref[...] + dot(dqb.astype(F32).T.astype(BF), xn)
        return carry

    lax.fori_loop(0, 4, chunk, 0)
    per = pieces // 4
    for r in range(4):
        back_refs[r][...] = back_all[r]
        for c in range(per):
            part = slice(c * CHUNK, c * CHUNK + CHUNK)
            to = lax.rem(z_at + OFFSETS[r], 4)
            both_ref[to, :width, part] = (dk_ref[r * per + c] * LN2).astype(BF)
            both_ref[to, width:, part] = dv_ref[r * per + c].astype(BF)
    gq_out[...] = (gq_ref[...] * norm).T.astype(BF)


def attend(norm, temper, xa_parts, xr_parts, up_parts, wq, kaug, vaug):
    rows = ANCH_DEV + xr_parts[0].shape[0]
    depth, width = wq.shape
    anchors = kaug.shape[0]
    vmem = pl.BlockSpec(memory_space=pltpu.VMEM)
    smem = pl.BlockSpec(memory_space=pltpu.SMEM)
    back = jax.ShapeDtypeStruct((rows, 2 * width), BF)
    both = jax.ShapeDtypeStruct((4, 2 * width, anchors // 4), BF)
    pieces = anchors // CHUNK
    outs = pl.pallas_call(
        functools.partial(attend_kernel, norm),
        out_shape=(back,) * 4 + (both,) + (jax.ShapeDtypeStruct((depth, width), BF),),
        in_specs=[smem] + [vmem] * 15,
        out_specs=(vmem,) * 6,
        scratch_shapes=[
            pltpu.VMEM((4, rows, depth), BF),
            pltpu.VMEM((4, rows, width), BF),
            pltpu.VMEM((4, FLAG_ROWS, width), F32),
            pltpu.VMEM((4, rows, 2 * width), BF),
            pltpu.VMEM((pieces, width, CHUNK), F32),
            pltpu.VMEM((pieces, width, CHUNK), F32),
            pltpu.VMEM((width, depth), F32),
            pltpu.VMEM((2, pieces, rows, CHUNK), BF),
        ],
        compiler_params=pltpu.CompilerParams(vmem_limit_bytes=56 * 1024 * 1024),
        cost_estimate=pl.CostEstimate(
            flops=14 * 4 * rows * anchors * width * 4,
            bytes_accessed=8 * 1024 * 1024,
            transcendentals=2 * 4 * rows * anchors,
        ),
    )(temper, *xa_parts, *xr_parts, *up_parts, wq, kaug, vaug)
    return outs[:4], outs[4], outs[5]


def tie(*values):
    return lax.optimization_barrier(values)


def shift(offset):
    return [(i, (i - offset) % 4) for i in range(4)]


def unshift(offset):
    return [(i, (i + offset) % 4) for i in range(4)]


def fan(values, axis, count):
    spread_out = jnp.broadcast_to(values[None], (count,) + values.shape)
    return lax.all_to_all(spread_out, axis, 0, 0)


def placed_at(parts, index):
    out = []
    for a in range(4):
        step = (index - a) % 4
        pick = parts[0]
        for r in (1, 2, 3):
            pick = jnp.where(step == OFFSETS[r], parts[r], pick)
        out.append(pick)
    return out


def columns(values, index, width):
    return lax.dynamic_slice_in_dim(values, index * width, width, 1)


def on_device(inputs, cotangent, flags, w_qkv, w_out, temper):
    x_at = lax.axis_index("x")
    z_at = lax.axis_index("zh")
    tokens = inputs[0]
    upstream_in = cotangent[0]
    inner = w_qkv.shape[1] // 3
    wide = inner // 4
    fsdp_count = lax.axis_size(FSDP)
    rows = tokens.shape[0]
    flag_rows = jnp.pad(
        flags[0].astype(BF),
        ((0, FLAG_ROWS - flags.shape[1]), (0, tokens.shape[1] - flags.shape[2])),
    )
    first = jnp.concatenate([tokens[:ANCH_DEV], flag_rows], axis=0)
    rest = tokens[ANCH_DEV:]
    xa_parts = [first] + [lax.ppermute(first, "x", shift(o)) for o in OFFSETS[1:]]
    width = tokens.shape[1]
    chosen = jnp.concatenate([columns(w_qkv, j * 4 + x_at, wide) for j in range(3)], axis=1)
    chosen = fan(chosen, FSDP, fsdp_count).reshape(-1, 3 * wide)
    lines = w_out.shape[0]
    chosen, mine = tie(chosen, w_out)
    projection = fan(mine, FSDP, fsdp_count).reshape(inner, width)

    *xa_parts, rest = tie(*xa_parts, rest)
    xr_parts = [rest] + [lax.ppermute(rest, "x", shift(o)) for o in OFFSETS[1:]]

    xa_f = jnp.concatenate([part[:ANCH_DEV] for part in xa_parts], axis=0).astype(F32)
    xa_n = (xa_f / row_scale(xa_f)).astype(BF)
    pair = dot(xa_n, chosen[:, wide:])
    lane = lax.broadcasted_iota(jnp.int32, (1, wide), 1)
    key = pair[:, :wide]
    k_inv = 1.0 / jnp.sqrt(pair_mean(key * key, lane) + EPS)
    k_norm = key * k_inv
    kv = jnp.concatenate([k_norm, pair[:, wide:]], axis=1).astype(BF)
    kv, xr_parts[1], xr_parts[2], ahead = tie(kv, xr_parts[1], xr_parts[2], upstream_in)
    kv_parts = [kv] + [lax.ppermute(kv, "zh", shift(o)) for o in OFFSETS[1:]]
    upstream = dot_nt(ahead, projection).astype(BF)
    up_parts = [columns(upstream, (x_at - o) % 4, wide) for o in OFFSETS]
    up_parts = [up_parts[0]] + [
        lax.ppermute(up_parts[i], "x", shift(OFFSETS[i])) for i in (1, 2, 3)
    ]
    *kv_parts, xr_parts[3], up_parts[1], up_parts[2], up_parts[3] = tie(
        *kv_parts, xr_parts[3], *up_parts[1:]
    )
    kv_all = jnp.concatenate(kv_parts, axis=0)
    anchors = kv_all.shape[0]
    place = lax.broadcasted_iota(jnp.int32, (anchors, wide), 0) // ANCH_DEV

    def turn(i):
        return jnp.where(i == 0, 0, jnp.where(i == 1, 3, i - 1))

    segment = (z_at + turn(place // 4)) % 4 * 4 + (x_at + turn(place % 4)) % 4
    column = lax.broadcasted_iota(jnp.int32, (anchors, wide), 1)
    kaug = jnp.concatenate([kv_all[:, :wide], (segment == column).astype(BF)], axis=1)
    vaug = jnp.concatenate([kv_all[:, wide:], (column < 2).astype(BF)], axis=1)
    kaug, w_mine = tie(kaug, w_qkv)
    weights = lax.all_gather(w_mine, FSDP, axis=0, tiled=True)

    count = rows * lax.axis_size(BLK) * fsdp_count
    norm = 1.0 / math.sqrt(count)
    backs, both, term_q = attend(
        norm, temper, xa_parts, xr_parts, up_parts, chosen[:, :wide], kaug, vaug
    )

    both = lax.all_to_all(both, "zh", 0, 0)
    sent = [backs[0]] + [lax.ppermute(backs[i], "x", unshift(OFFSETS[i])) for i in (1, 2, 3)]
    sent = placed_at(sent, x_at)
    attended = jnp.concatenate([part[:, :wide] for part in sent], axis=1)
    dqb = jnp.concatenate([part[:, wide:] for part in sent], axis=1)
    term_out = lax.dot_general(
        attended, upstream_in, (((0,), (0,)), ((), ())), preferred_element_type=F32
    )
    term_out = (term_out * norm).reshape(fsdp_count, 4, -1, width)
    pieces = [
        lax.dynamic_index_in_dim(term_out, (x_at + o) % 4, 1, keepdims=False) for o in OFFSETS
    ]
    term_out = pieces[0]
    for i in (1, 2, 3):
        term_out += lax.ppermute(pieces[i].astype(BF), "x", unshift(OFFSETS[i])).astype(F32)
    term_out = term_out.astype(BF)
    both, term_out = tie(both, term_out)

    total = jnp.sum(both.astype(F32), axis=0)
    total = total.T
    dkn = total[:, :wide]
    dkb = (dkn - k_norm * pair_mean(dkn * k_norm, lane)) * k_inv
    dkv = jnp.concatenate([dkb, total[:, wide:]], axis=1).astype(BF)
    term_kv = lax.dot_general(xa_n, dkv, (((0,), (0,)), ((), ())), preferred_element_type=F32)
    term_kv = (term_kv * norm).astype(BF).reshape(fsdp_count, -1, width)
    late = [term_out, term_q.reshape(fsdp_count, -1, width), term_kv]
    late = lax.all_to_all(jnp.concatenate(late, axis=1), FSDP, 0, 0)
    dkv_parts = [dkv[:ANCH_DEV]] + [
        lax.ppermute(dkv[i * ANCH_DEV : (i + 1) * ANCH_DEV], "x", unshift(OFFSETS[i]))
        for i in (1, 2, 3)
    ]
    dkv_parts = placed_at(dkv_parts, x_at)
    xf = tokens.astype(F32)
    scale = row_scale(xf)
    normed = xf / scale
    output = (xf + dot(attended, projection)).astype(BF)
    d_normed = dot_nt(dqb, weights[:, :inner])
    d_pair = jnp.concatenate(
        [part[:, :wide] for part in dkv_parts] + [part[:, wide:] for part in dkv_parts], axis=1
    )
    d_normed = d_normed.at[:ANCH_DEV].add(dot_nt(d_pair, weights[:, inner:]))
    mean = jnp.mean(d_normed * normed, axis=-1, keepdims=True)
    grad_in = (upstream_in.astype(F32) + (d_normed - normed * mean) / scale).astype(BF)

    late, grad_in, output = tie(late, grad_in, output)
    late = jnp.sum(late.astype(F32), axis=0).astype(BF)
    late_parts = [late] + [lax.ppermute(late, "zh", shift(o)) for o in OFFSETS[1:]]
    late = sum(part.astype(F32) for part in late_parts).astype(BF)
    late_parts = [late] + [lax.ppermute(late, "x", unshift(o)) for o in OFFSETS[1:]]
    late_parts = placed_at([part.astype(F32) for part in late_parts], x_at)
    lines = lines // 4
    grad_out = jnp.concatenate([part[:lines] for part in late_parts], axis=0)
    late_parts = [part[lines:] for part in late_parts]
    share = w_qkv.shape[0]
    deep = wide * share // width
    part_q = [part[:deep].reshape(share, wide) for part in late_parts]
    part_kv = [part[deep:].reshape(share, 2 * wide) for part in late_parts]
    grad_qkv = jnp.concatenate(
        part_q + [part[:, :wide] for part in part_kv] + [part[:, wide:] for part in part_kv],
        axis=1,
    )
    return (output[None], grad_in[None], grad_qkv, grad_out)


def solution(mesh):
    split = Mesh(mesh.devices.reshape(4, 4, 2, 4, 2), BLK + FSDP)
    placed = (
        P(FSDP, BLK, None),
        P(FSDP, BLK, None),
        P(FSDP, BLK, None),
        P(FSDP, None),
        P(FSDP, None),
        P(),
    )
    return jax.shard_map(
        on_device,
        mesh=split,
        in_specs=placed,
        out_specs=(
            P(FSDP, BLK, None),
            P(FSDP, BLK, None),
            P(FSDP, None),
            P(FSDP, None),
        ),
        check_vma=False,
    )
```

```python
import functools
import math

import jax
import jax.numpy as jnp
from jax import lax
from jax.experimental import pallas as pl
from jax.experimental.pallas import tpu as pltpu
from jax.sharding import Mesh, PartitionSpec as P

HEADS = 8
HD = 64
BLOCK = 128
ANCH_DEV = 128
EPS = 1e-06
FLAG_ROWS = 16
LOG2E = math.log2(math.e)
LN2 = math.log(2.0)
OFFSETS = (0, 3, 1, 2)
FSDP = ("zl", "y", "c")
BLK = ("zh", "x")
BF = jnp.bfloat16
F32 = jnp.float32
CHUNK = 256


def dot(a, b):
    return jnp.dot(a, b, preferred_element_type=F32)


def dot_nt(a, b):
    return lax.dot_general(a, b, (((1,), (1,)), ((), ())), preferred_element_type=F32)


def row_scale(values):
    return jnp.sqrt(jnp.mean(values * values, axis=-1, keepdims=True) + EPS)


def spread(left, right, lane):
    return jnp.where(lane < HD, left, right)


def pair_mean(values, lane):
    left = jnp.sum(jnp.where(lane < HD, values, 0.0), axis=-1, keepdims=True)
    right = jnp.sum(jnp.where(lane < HD, 0.0, values), axis=-1, keepdims=True)
    return spread(left, right, lane) * (1.0 / HD)


def attend_kernel(norm, *refs):
    temper_ref, *refs = refs
    xa_refs, xr_refs, refs = refs[:4], refs[4:8], refs[8:]
    up_refs, refs = refs[:4], refs[4:]
    wq_ref, kaug_ref, vaug_ref, *refs = refs
    back_refs, both_ref, refs = refs[:4], refs[4], refs[5:]
    gq_out, xn_ref, u_ref, mask_ref, back_all, dk_ref, dv_ref, gq_ref, exp_ref = refs
    x_at = lax.axis_index("x")
    z_at = lax.axis_index("zh")
    rows = xn_ref.shape[1]
    width = wq_ref.shape[1]
    pieces = dk_ref.shape[0]
    for r in range(4):
        u_ref[r] = up_refs[r][...]
        for lo, ref in ((0, xa_refs[r]), (ANCH_DEV, xr_refs[r])):
            for start in range(0, rows - ANCH_DEV if lo else ANCH_DEV, BLOCK):
                xf = ref[start : start + BLOCK, :].astype(F32)
                xn_ref[r, lo + start : lo + start + BLOCK, :] = (xf / row_scale(xf)).astype(BF)
        flag_rows = xa_refs[r][ANCH_DEV : ANCH_DEV + FLAG_ROWS, :width].astype(F32)
        mask_ref[r] = jnp.where(flag_rows > 0.0, 0.0, -1024.0)
    dk_ref[...] = jnp.zeros_like(dk_ref)
    dv_ref[...] = jnp.zeros_like(dv_ref)
    gq_ref[...] = jnp.zeros_like(gq_ref)
    lane = lax.broadcasted_iota(jnp.int32, (rows, width), 1)
    first = x_at * 2
    f_left = temper_ref[first] * (1.0 / math.sqrt(HD))
    f_right = temper_ref[first + 1] * (1.0 / math.sqrt(HD))
    factor = spread(f_left, f_right, lane)

    def chunk(i, carry):
        xn = xn_ref[i]
        query = dot(xn, wq_ref[...])
        q_inv = 1.0 / jnp.sqrt(pair_mean(query * query, lane) + EPS)
        q_norm = query * q_inv
        q_bf = (q_norm * (factor * LOG2E)).astype(BF)
        q_t = q_bf.astype(F32).T.astype(BF)
        up = u_ref[i]
        up_t = up.astype(F32).T.astype(BF)
        mask_rows = mask_ref[i]
        mask = jnp.concatenate(
            [
                jnp.broadcast_to(mask_rows[j : j + 1, :], (BLOCK, width))
                for j in range(rows // BLOCK)
            ],
            axis=0,
        ).astype(BF)
        out = jnp.zeros((rows, width), F32)
        dqn = jnp.zeros((rows, width), F32)
        for head in range(2):
            sel = (lane < HD) if head == 0 else (lane >= HD)
            span = slice(head * HD, head * HD + HD)
            q_aug = jnp.concatenate([jnp.where(sel, q_bf, 0), mask], axis=1)
            acc = jnp.zeros((rows, 2 * width), F32)
            for c in range(pieces):
                part = slice(c * CHUNK, c * CHUNK + CHUNK)
                expo = jnp.exp2(dot_nt(q_aug, kaug_ref[part, :])).astype(BF)
                exp_ref[head, c] = expo
                acc = acc + dot(expo, vaug_ref[part, :])
            inv = 1.0 / acc[:, width : width + 1]
            out_h = acc[:, :width] * inv
            out = jnp.where(sel, out_h, out)
            u_h = jnp.where(sel, up, 0)
            delta = -jnp.sum(out_h * u_h.astype(F32), axis=1, keepdims=True)
            d_hi = delta.astype(BF).astype(F32)
            tail = jnp.where(lane == 0, d_hi, jnp.where(lane == 1, delta - d_hi, 0.0))
            u_aug = jnp.concatenate([u_h, tail.astype(BF)], axis=1)
            dq_h = jnp.zeros((rows, width), F32)
            for c in range(pieces):
                part = slice(c * CHUNK, c * CHUNK + CHUNK)
                dp = dot_nt(u_aug, vaug_ref[part, :])
                prob = exp_ref[head, c].astype(F32) * inv
                dz = (prob * dp).astype(BF)
                dq_h = dq_h + dot(dz, kaug_ref[part, :width])
                dk_ref[c, span, :] = dk_ref[c, span, :] + dot(q_t[span, :], dz)
                dv_ref[c, span, :] = dv_ref[c, span, :] + dot(up_t[span, :], prob.astype(BF))
            dqn = jnp.where(sel, dq_h, dqn)
        dqn = dqn * factor
        dqb = ((dqn - q_norm * pair_mean(dqn * q_norm, lane)) * q_inv).astype(BF)
        back_all[i, :, :width] = out.astype(BF)
        back_all[i, :, width:] = dqb
        gq_ref[...] = gq_ref[...] + dot(dqb.astype(F32).T.astype(BF), xn)
        return carry

    lax.fori_loop(0, 4, chunk, 0)
    per = pieces // 4
    for r in range(4):
        back_refs[r][...] = back_all[r]
        for c in range(per):
            part = slice(c * CHUNK, c * CHUNK + CHUNK)
            to = lax.rem(z_at + OFFSETS[r], 4)
            both_ref[to, :width, part] = (dk_ref[r * per + c] * LN2).astype(BF)
            both_ref[to, width:, part] = dv_ref[r * per + c].astype(BF)
    gq_out[...] = (gq_ref[...] * norm).T.astype(BF)


def attend(norm, temper, xa_parts, xr_parts, up_parts, wq, kaug, vaug):
    rows = ANCH_DEV + xr_parts[0].shape[0]
    depth, width = wq.shape
    anchors = kaug.shape[0]
    vmem = pl.BlockSpec(memory_space=pltpu.VMEM)
    smem = pl.BlockSpec(memory_space=pltpu.SMEM)
    back = jax.ShapeDtypeStruct((rows, 2 * width), BF)
    both = jax.ShapeDtypeStruct((4, 2 * width, anchors // 4), BF)
    pieces = anchors // CHUNK
    outs = pl.pallas_call(
        functools.partial(attend_kernel, norm),
        out_shape=(back,) * 4 + (both,) + (jax.ShapeDtypeStruct((depth, width), BF),),
        in_specs=[smem] + [vmem] * 15,
        out_specs=(vmem,) * 6,
        scratch_shapes=[
            pltpu.VMEM((4, rows, depth), BF),
            pltpu.VMEM((4, rows, width), BF),
            pltpu.VMEM((4, FLAG_ROWS, width), F32),
            pltpu.VMEM((4, rows, 2 * width), BF),
            pltpu.VMEM((pieces, width, CHUNK), F32),
            pltpu.VMEM((pieces, width, CHUNK), F32),
            pltpu.VMEM((width, depth), F32),
            pltpu.VMEM((2, pieces, rows, CHUNK), BF),
        ],
        compiler_params=pltpu.CompilerParams(vmem_limit_bytes=56 * 1024 * 1024),
        cost_estimate=pl.CostEstimate(
            flops=14 * 4 * rows * anchors * width * 4,
            bytes_accessed=8 * 1024 * 1024,
            transcendentals=2 * 4 * rows * anchors,
        ),
    )(temper, *xa_parts, *xr_parts, *up_parts, wq, kaug, vaug)
    return outs[:4], outs[4], outs[5]


def tie(*values):
    return lax.optimization_barrier(values)


def shift(offset):
    return [(i, (i - offset) % 4) for i in range(4)]


def unshift(offset):
    return [(i, (i + offset) % 4) for i in range(4)]


def fan(values, axis, count):
    spread_out = jnp.broadcast_to(values[None], (count,) + values.shape)
    return lax.all_to_all(spread_out, axis, 0, 0)


def placed_at(parts, index):
    out = []
    for a in range(4):
        step = (index - a) % 4
        pick = parts[0]
        for r in (1, 2, 3):
            pick = jnp.where(step == OFFSETS[r], parts[r], pick)
        out.append(pick)
    return out


def columns(values, index, width):
    return lax.dynamic_slice_in_dim(values, index * width, width, 1)


def on_device(inputs, cotangent, flags, w_qkv, w_out, temper):
    x_at = lax.axis_index("x")
    z_at = lax.axis_index("zh")
    tokens = inputs[0]
    upstream_in = cotangent[0]
    inner = w_qkv.shape[1] // 3
    wide = inner // 4
    fsdp_count = lax.axis_size(FSDP)
    rows = tokens.shape[0]
    flag_rows = jnp.pad(
        flags[0].astype(BF),
        ((0, FLAG_ROWS - flags.shape[1]), (0, tokens.shape[1] - flags.shape[2])),
    )
    first = jnp.concatenate([tokens[:ANCH_DEV], flag_rows], axis=0)
    rest = tokens[ANCH_DEV:]
    xa_parts = [first] + [lax.ppermute(first, "x", shift(o)) for o in OFFSETS[1:]]
    width = tokens.shape[1]
    chosen = jnp.concatenate([columns(w_qkv, j * 4 + x_at, wide) for j in range(3)], axis=1)
    chosen = fan(chosen, FSDP, fsdp_count).reshape(-1, 3 * wide)
    lines = w_out.shape[0]
    chosen, mine = tie(chosen, w_out)
    projection = fan(mine, FSDP, fsdp_count).reshape(inner, width)

    *xa_parts, rest = tie(*xa_parts, rest)
    xr_parts = [rest] + [lax.ppermute(rest, "x", shift(o)) for o in OFFSETS[1:]]

    xa_f = jnp.concatenate([part[:ANCH_DEV] for part in xa_parts], axis=0).astype(F32)
    xa_n = (xa_f / row_scale(xa_f)).astype(BF)
    pair = dot(xa_n, chosen[:, wide:])
    lane = lax.broadcasted_iota(jnp.int32, (1, wide), 1)
    key = pair[:, :wide]
    k_inv = 1.0 / jnp.sqrt(pair_mean(key * key, lane) + EPS)
    k_norm = key * k_inv
    kv = jnp.concatenate([k_norm, pair[:, wide:]], axis=1).astype(BF)
    kv, xr_parts[1], ahead = tie(kv, xr_parts[1], upstream_in)
    kv_parts = [kv] + [lax.ppermute(kv, "zh", shift(o)) for o in OFFSETS[1:]]
    upstream = dot_nt(ahead, projection).astype(BF)
    up_parts = [columns(upstream, (x_at - o) % 4, wide) for o in OFFSETS]
    up_parts = [up_parts[0]] + [
        lax.ppermute(up_parts[i], "x", shift(OFFSETS[i])) for i in (1, 2, 3)
    ]
    *kv_parts, xr_parts[2], xr_parts[3], up_parts[1], up_parts[2], up_parts[3] = tie(
        *kv_parts, xr_parts[2], xr_parts[3], *up_parts[1:]
    )
    kv_all = jnp.concatenate(kv_parts, axis=0)
    anchors = kv_all.shape[0]
    place = lax.broadcasted_iota(jnp.int32, (anchors, wide), 0) // ANCH_DEV

    def turn(i):
        return jnp.where(i == 0, 0, jnp.where(i == 1, 3, i - 1))

    segment = (z_at + turn(place // 4)) % 4 * 4 + (x_at + turn(place % 4)) % 4
    column = lax.broadcasted_iota(jnp.int32, (anchors, wide), 1)
    kaug = jnp.concatenate([kv_all[:, :wide], (segment == column).astype(BF)], axis=1)
    vaug = jnp.concatenate([kv_all[:, wide:], (column < 2).astype(BF)], axis=1)
    kaug, w_mine = tie(kaug, w_qkv)
    weights = lax.all_gather(w_mine, FSDP, axis=0, tiled=True)

    count = rows * lax.axis_size(BLK) * fsdp_count
    norm = 1.0 / math.sqrt(count)
    backs, both, term_q = attend(
        norm, temper, xa_parts, xr_parts, up_parts, chosen[:, :wide], kaug, vaug
    )

    both = lax.all_to_all(both, "zh", 0, 0)
    sent = [backs[0]] + [lax.ppermute(backs[i], "x", unshift(OFFSETS[i])) for i in (1, 2, 3)]
    sent = placed_at(sent, x_at)
    attended = jnp.concatenate([part[:, :wide] for part in sent], axis=1)
    dqb = jnp.concatenate([part[:, wide:] for part in sent], axis=1)
    term_out = lax.dot_general(
        attended, upstream_in, (((0,), (0,)), ((), ())), preferred_element_type=F32
    )
    term_out = (term_out * norm).reshape(fsdp_count, 4, -1, width)
    pieces = [
        lax.dynamic_index_in_dim(term_out, (x_at + o) % 4, 1, keepdims=False) for o in OFFSETS
    ]
    term_out = pieces[0]
    for i in (1, 2, 3):
        term_out += lax.ppermute(pieces[i].astype(BF), "x", unshift(OFFSETS[i])).astype(F32)
    term_out = term_out.astype(BF)
    both, term_out = tie(both, term_out)

    total = jnp.sum(both.astype(F32), axis=0)
    total = total.T
    dkn = total[:, :wide]
    dkb = (dkn - k_norm * pair_mean(dkn * k_norm, lane)) * k_inv
    dkv = jnp.concatenate([dkb, total[:, wide:]], axis=1).astype(BF)
    term_kv = lax.dot_general(xa_n, dkv, (((0,), (0,)), ((), ())), preferred_element_type=F32)
    term_kv = (term_kv * norm).astype(BF).reshape(fsdp_count, -1, width)
    late = [term_out, term_q.reshape(fsdp_count, -1, width), term_kv]
    late = lax.all_to_all(jnp.concatenate(late, axis=1), FSDP, 0, 0)
    dkv_parts = [dkv[:ANCH_DEV]] + [
        lax.ppermute(dkv[i * ANCH_DEV : (i + 1) * ANCH_DEV], "x", unshift(OFFSETS[i]))
        for i in (1, 2, 3)
    ]
    dkv_parts = placed_at(dkv_parts, x_at)
    xf = tokens.astype(F32)
    scale = row_scale(xf)
    normed = xf / scale
    output = (xf + dot(attended, projection)).astype(BF)
    d_normed = dot_nt(dqb, weights[:, :inner])
    d_pair = jnp.concatenate(
        [part[:, :wide] for part in dkv_parts] + [part[:, wide:] for part in dkv_parts], axis=1
    )
    d_normed = d_normed.at[:ANCH_DEV].add(dot_nt(d_pair, weights[:, inner:]))
    mean = jnp.mean(d_normed * normed, axis=-1, keepdims=True)
    grad_in = (upstream_in.astype(F32) + (d_normed - normed * mean) / scale).astype(BF)

    late, grad_in, output = tie(late, grad_in, output)
    late = jnp.sum(late.astype(F32), axis=0).astype(BF)
    late_parts = [late] + [lax.ppermute(late, "zh", shift(o)) for o in OFFSETS[1:]]
    late = sum(part.astype(F32) for part in late_parts).astype(BF)
    late_parts = [late] + [lax.ppermute(late, "x", unshift(o)) for o in OFFSETS[1:]]
    late_parts = placed_at([part.astype(F32) for part in late_parts], x_at)
    lines = lines // 4
    grad_out = jnp.concatenate([part[:lines] for part in late_parts], axis=0)
    late_parts = [part[lines:] for part in late_parts]
    share = w_qkv.shape[0]
    deep = wide * share // width
    part_q = [part[:deep].reshape(share, wide) for part in late_parts]
    part_kv = [part[deep:].reshape(share, 2 * wide) for part in late_parts]
    grad_qkv = jnp.concatenate(
        part_q + [part[:, :wide] for part in part_kv] + [part[:, wide:] for part in part_kv],
        axis=1,
    )
    return (output[None], grad_in[None], grad_qkv, grad_out)


def solution(mesh):
    split = Mesh(mesh.devices.reshape(4, 4, 2, 4, 2), BLK + FSDP)
    placed = (
        P(FSDP, BLK, None),
        P(FSDP, BLK, None),
        P(FSDP, BLK, None),
        P(FSDP, None),
        P(FSDP, None),
        P(),
    )
    return jax.shard_map(
        on_device,
        mesh=split,
        in_specs=placed,
        out_specs=(
            P(FSDP, BLK, None),
            P(FSDP, BLK, None),
            P(FSDP, None),
            P(FSDP, None),
        ),
        check_vma=False,
    )
```

```python
import functools
import math

import jax
import jax.numpy as jnp
from jax import lax
from jax.experimental import pallas as pl
from jax.experimental.pallas import tpu as pltpu
from jax.sharding import Mesh, PartitionSpec as P

HEADS = 8
HD = 64
BLOCK = 128
ANCH_DEV = 128
EPS = 1e-06
FLAG_ROWS = 16
LOG2E = math.log2(math.e)
LN2 = math.log(2.0)
OFFSETS = (0, 3, 1, 2)
FSDP = ("zl", "y", "c")
BLK = ("zh", "x")
BF = jnp.bfloat16
F32 = jnp.float32
CHUNK = 2048


def dot(a, b):
    return jnp.dot(a, b, preferred_element_type=F32)


def dot_nt(a, b):
    return lax.dot_general(a, b, (((1,), (1,)), ((), ())), preferred_element_type=F32)


def row_scale(values):
    return jnp.sqrt(jnp.mean(values * values, axis=-1, keepdims=True) + EPS)


def spread(left, right, lane):
    return jnp.where(lane < HD, left, right)


def pair_mean(values, lane):
    left = jnp.sum(jnp.where(lane < HD, values, 0.0), axis=-1, keepdims=True)
    right = jnp.sum(jnp.where(lane < HD, 0.0, values), axis=-1, keepdims=True)
    return spread(left, right, lane) * (1.0 / HD)


def attend_kernel(norm, *refs):
    temper_ref, *refs = refs
    xa_refs, xr_refs, refs = refs[:4], refs[4:8], refs[8:]
    up_refs, refs = refs[:4], refs[4:]
    wq_ref, kaug_ref, vaug_ref, *refs = refs
    back_refs, both_ref, refs = refs[:4], refs[4], refs[5:]
    gq_out, xn_ref, u_ref, mask_ref, back_all, dk_ref, dv_ref, gq_ref, exp_ref = refs
    x_at = lax.axis_index("x")
    z_at = lax.axis_index("zh")
    rows = xn_ref.shape[1]
    width = wq_ref.shape[1]
    pieces = dk_ref.shape[0]
    for r in range(4):
        u_ref[r] = up_refs[r][...]
        for lo, ref in ((0, xa_refs[r]), (ANCH_DEV, xr_refs[r])):
            for start in range(0, rows - ANCH_DEV if lo else ANCH_DEV, BLOCK):
                xf = ref[start : start + BLOCK, :].astype(F32)
                xn_ref[r, lo + start : lo + start + BLOCK, :] = (xf / row_scale(xf)).astype(BF)
        flag_rows = xa_refs[r][ANCH_DEV : ANCH_DEV + FLAG_ROWS, :width].astype(F32)
        mask_ref[r] = jnp.where(flag_rows > 0.0, 0.0, -1024.0)
    dk_ref[...] = jnp.zeros_like(dk_ref)
    dv_ref[...] = jnp.zeros_like(dv_ref)
    gq_ref[...] = jnp.zeros_like(gq_ref)
    lane = lax.broadcasted_iota(jnp.int32, (rows, width), 1)
    first = x_at * 2
    f_left = temper_ref[first] * (1.0 / math.sqrt(HD))
    f_right = temper_ref[first + 1] * (1.0 / math.sqrt(HD))
    factor = spread(f_left, f_right, lane)

    def chunk(i, carry):
        xn = xn_ref[i]
        query = dot(xn, wq_ref[...])
        q_inv = 1.0 / jnp.sqrt(pair_mean(query * query, lane) + EPS)
        q_norm = query * q_inv
        q_bf = (q_norm * (factor * LOG2E)).astype(BF)
        q_t = q_bf.astype(F32).T.astype(BF)
        up = u_ref[i]
        up_t = up.astype(F32).T.astype(BF)
        mask_rows = mask_ref[i]
        mask = jnp.concatenate(
            [
                jnp.broadcast_to(mask_rows[j : j + 1, :], (BLOCK, width))
                for j in range(rows // BLOCK)
            ],
            axis=0,
        ).astype(BF)
        sels = [lane < HD, lane >= HD]
        q_aug = [jnp.concatenate([jnp.where(sel, q_bf, 0), mask], axis=1) for sel in sels]
        acc = [jnp.zeros((rows, 2 * width), F32)] * 2
        dq = [jnp.zeros((rows, width), F32)] * 2
        u_aug, inv, outs = [None] * 2, [None] * 2, [None] * 2

        def forward(head, c):
            part = slice(c * CHUNK, c * CHUNK + CHUNK)
            expo = jnp.exp2(dot_nt(q_aug[head], kaug_ref[part, :])).astype(BF)
            exp_ref[head, c] = expo
            acc[head] = acc[head] + dot(expo, vaug_ref[part, :])

        def middle(head):
            inv[head] = 1.0 / acc[head][:, width : width + 1]
            outs[head] = acc[head][:, :width] * inv[head]
            u_h = jnp.where(sels[head], up, 0)
            delta = -jnp.sum(outs[head] * u_h.astype(F32), axis=1, keepdims=True)
            d_hi = delta.astype(BF).astype(F32)
            tail = jnp.where(lane == 0, d_hi, jnp.where(lane == 1, delta - d_hi, 0.0))
            u_aug[head] = jnp.concatenate([u_h, tail.astype(BF)], axis=1)

        def backward(head, c):
            span = slice(head * HD, head * HD + HD)
            part = slice(c * CHUNK, c * CHUNK + CHUNK)
            dp = dot_nt(u_aug[head], vaug_ref[part, :])
            prob = exp_ref[head, c].astype(F32) * inv[head]
            dz = (prob * dp).astype(BF)
            dq[head] = dq[head] + dot(dz, kaug_ref[part, :width])
            dk_ref[c, span, :] = dk_ref[c, span, :] + dot(q_t[span, :], dz)
            dv_ref[c, span, :] = dv_ref[c, span, :] + dot(up_t[span, :], prob.astype(BF))

        for head in range(2):
            for c in range(pieces):
                forward(head, c)
            middle(head)
        for head in range(2):
            for c in range(pieces):
                backward(head, c)
        out = jnp.where(sels[0], outs[0], outs[1])
        dqn = jnp.where(sels[0], dq[0], dq[1])
        dqn = dqn * factor
        dqb = ((dqn - q_norm * pair_mean(dqn * q_norm, lane)) * q_inv).astype(BF)
        back_all[i, :, :width] = out.astype(BF)
        back_all[i, :, width:] = dqb
        gq_ref[...] = gq_ref[...] + dot(dqb.astype(F32).T.astype(BF), xn)
        return carry

    lax.fori_loop(0, 4, chunk, 0)
    share = both_ref.shape[2]
    for r in range(4):
        back_refs[r][...] = back_all[r]
        to = lax.rem(z_at + OFFSETS[r], 4)
        c, lo = divmod(r * share, CHUNK)
        both_ref[to, :width, :] = (dk_ref[c, :, lo : lo + share] * LN2).astype(BF)
        both_ref[to, width:, :] = dv_ref[c, :, lo : lo + share].astype(BF)
    gq_out[...] = (gq_ref[...] * norm).T.astype(BF)


def attend(norm, temper, xa_parts, xr_parts, up_parts, wq, kaug, vaug):
    rows = ANCH_DEV + xr_parts[0].shape[0]
    depth, width = wq.shape
    anchors = kaug.shape[0]
    vmem = pl.BlockSpec(memory_space=pltpu.VMEM)
    smem = pl.BlockSpec(memory_space=pltpu.SMEM)
    back = jax.ShapeDtypeStruct((rows, 2 * width), BF)
    both = jax.ShapeDtypeStruct((4, 2 * width, anchors // 4), BF)
    pieces = anchors // CHUNK
    outs = pl.pallas_call(
        functools.partial(attend_kernel, norm),
        out_shape=(back,) * 4 + (both,) + (jax.ShapeDtypeStruct((depth, width), BF),),
        in_specs=[smem] + [vmem] * 15,
        out_specs=(vmem,) * 6,
        scratch_shapes=[
            pltpu.VMEM((4, rows, depth), BF),
            pltpu.VMEM((4, rows, width), BF),
            pltpu.VMEM((4, FLAG_ROWS, width), F32),
            pltpu.VMEM((4, rows, 2 * width), BF),
            pltpu.VMEM((pieces, width, CHUNK), F32),
            pltpu.VMEM((pieces, width, CHUNK), F32),
            pltpu.VMEM((width, depth), F32),
            pltpu.VMEM((2, pieces, rows, CHUNK), BF),
        ],
        compiler_params=pltpu.CompilerParams(vmem_limit_bytes=56 * 1024 * 1024),
        cost_estimate=pl.CostEstimate(
            flops=14 * 4 * rows * anchors * width * 4,
            bytes_accessed=8 * 1024 * 1024,
            transcendentals=2 * 4 * rows * anchors,
        ),
    )(temper, *xa_parts, *xr_parts, *up_parts, wq, kaug, vaug)
    return outs[:4], outs[4], outs[5]


def tie(*values):
    return lax.optimization_barrier(values)


def shift(offset):
    return [(i, (i - offset) % 4) for i in range(4)]


def unshift(offset):
    return [(i, (i + offset) % 4) for i in range(4)]


def fan(values, axis, count):
    spread_out = jnp.broadcast_to(values[None], (count,) + values.shape)
    return lax.all_to_all(spread_out, axis, 0, 0)


def placed_at(parts, index):
    out = []
    for a in range(4):
        step = (index - a) % 4
        pick = parts[0]
        for r in (1, 2, 3):
            pick = jnp.where(step == OFFSETS[r], parts[r], pick)
        out.append(pick)
    return out


def columns(values, index, width):
    return lax.dynamic_slice_in_dim(values, index * width, width, 1)


def on_device(inputs, cotangent, flags, w_qkv, w_out, temper):
    x_at = lax.axis_index("x")
    z_at = lax.axis_index("zh")
    tokens = inputs[0]
    upstream_in = cotangent[0]
    inner = w_qkv.shape[1] // 3
    wide = inner // 4
    fsdp_count = lax.axis_size(FSDP)
    rows = tokens.shape[0]
    flag_rows = jnp.pad(
        flags[0].astype(BF),
        ((0, FLAG_ROWS - flags.shape[1]), (0, tokens.shape[1] - flags.shape[2])),
    )
    first = jnp.concatenate([tokens[:ANCH_DEV], flag_rows], axis=0)
    rest = tokens[ANCH_DEV:]
    xa_parts = [first] + [lax.ppermute(first, "x", shift(o)) for o in OFFSETS[1:]]
    width = tokens.shape[1]
    chosen = jnp.concatenate([columns(w_qkv, j * 4 + x_at, wide) for j in range(3)], axis=1)
    chosen = fan(chosen, FSDP, fsdp_count).reshape(-1, 3 * wide)
    lines = w_out.shape[0]
    chosen, mine = tie(chosen, w_out)
    projection = fan(mine, FSDP, fsdp_count).reshape(inner, width)

    *xa_parts, rest = tie(*xa_parts, rest)
    xr_parts = [rest] + [lax.ppermute(rest, "x", shift(o)) for o in OFFSETS[1:]]

    xa_f = jnp.concatenate([part[:ANCH_DEV] for part in xa_parts], axis=0).astype(F32)
    xa_n = (xa_f / row_scale(xa_f)).astype(BF)
    pair = dot(xa_n, chosen[:, wide:])
    lane = lax.broadcasted_iota(jnp.int32, (1, wide), 1)
    key = pair[:, :wide]
    k_inv = 1.0 / jnp.sqrt(pair_mean(key * key, lane) + EPS)
    k_norm = key * k_inv
    kv = jnp.concatenate([k_norm, pair[:, wide:]], axis=1).astype(BF)
    kv, xr_parts[1], xr_parts[2], ahead = tie(kv, xr_parts[1], xr_parts[2], upstream_in)
    kv_parts = [kv] + [lax.ppermute(kv, "zh", shift(o)) for o in OFFSETS[1:]]
    upstream = dot_nt(ahead, projection).astype(BF)
    up_parts = [columns(upstream, (x_at - o) % 4, wide) for o in OFFSETS]
    up_parts = [up_parts[0]] + [
        lax.ppermute(up_parts[i], "x", shift(OFFSETS[i])) for i in (1, 2, 3)
    ]
    *kv_parts, xr_parts[3], up_parts[1], up_parts[2], up_parts[3] = tie(
        *kv_parts, xr_parts[3], *up_parts[1:]
    )
    kv_all = jnp.concatenate(kv_parts, axis=0)
    anchors = kv_all.shape[0]
    place = lax.broadcasted_iota(jnp.int32, (anchors, wide), 0) // ANCH_DEV

    def turn(i):
        return jnp.where(i == 0, 0, jnp.where(i == 1, 3, i - 1))

    segment = (z_at + turn(place // 4)) % 4 * 4 + (x_at + turn(place % 4)) % 4
    column = lax.broadcasted_iota(jnp.int32, (anchors, wide), 1)
    kaug = jnp.concatenate([kv_all[:, :wide], (segment == column).astype(BF)], axis=1)
    vaug = jnp.concatenate([kv_all[:, wide:], (column < 2).astype(BF)], axis=1)
    kaug, w_mine = tie(kaug, w_qkv)
    weights = lax.all_gather(w_mine, FSDP, axis=0, tiled=True)

    count = rows * lax.axis_size(BLK) * fsdp_count
    norm = 1.0 / math.sqrt(count)
    backs, both, term_q = attend(
        norm, temper, xa_parts, xr_parts, up_parts, chosen[:, :wide], kaug, vaug
    )

    both = lax.all_to_all(both, "zh", 0, 0)
    sent = [backs[0]] + [lax.ppermute(backs[i], "x", unshift(OFFSETS[i])) for i in (1, 2, 3)]
    sent = placed_at(sent, x_at)
    attended = jnp.concatenate([part[:, :wide] for part in sent], axis=1)
    dqb = jnp.concatenate([part[:, wide:] for part in sent], axis=1)
    term_out = lax.dot_general(
        attended, upstream_in, (((0,), (0,)), ((), ())), preferred_element_type=F32
    )
    term_out = (term_out * norm).reshape(fsdp_count, 4, -1, width)
    pieces = [
        lax.dynamic_index_in_dim(term_out, (x_at + o) % 4, 1, keepdims=False) for o in OFFSETS
    ]
    term_out = pieces[0]
    for i in (1, 2, 3):
        term_out += lax.ppermute(pieces[i].astype(BF), "x", unshift(OFFSETS[i])).astype(F32)
    term_out = term_out.astype(BF)
    both, term_out = tie(both, term_out)

    total = jnp.sum(both.astype(F32), axis=0)
    total = total.T
    dkn = total[:, :wide]
    dkb = (dkn - k_norm * pair_mean(dkn * k_norm, lane)) * k_inv
    dkv = jnp.concatenate([dkb, total[:, wide:]], axis=1).astype(BF)
    term_kv = lax.dot_general(xa_n, dkv, (((0,), (0,)), ((), ())), preferred_element_type=F32)
    term_kv = (term_kv * norm).astype(BF).reshape(fsdp_count, -1, width)
    late = [term_out, term_q.reshape(fsdp_count, -1, width), term_kv]
    late = lax.all_to_all(jnp.concatenate(late, axis=1), FSDP, 0, 0)
    dkv_parts = [dkv[:ANCH_DEV]] + [
        lax.ppermute(dkv[i * ANCH_DEV : (i + 1) * ANCH_DEV], "x", unshift(OFFSETS[i]))
        for i in (1, 2, 3)
    ]
    dkv_parts = placed_at(dkv_parts, x_at)
    xf = tokens.astype(F32)
    scale = row_scale(xf)
    normed = xf / scale
    output = (xf + dot(attended, projection)).astype(BF)
    d_normed = dot_nt(dqb, weights[:, :inner])
    d_pair = jnp.concatenate(
        [part[:, :wide] for part in dkv_parts] + [part[:, wide:] for part in dkv_parts], axis=1
    )
    d_normed = d_normed.at[:ANCH_DEV].add(dot_nt(d_pair, weights[:, inner:]))
    mean = jnp.mean(d_normed * normed, axis=-1, keepdims=True)
    grad_in = (upstream_in.astype(F32) + (d_normed - normed * mean) / scale).astype(BF)

    late, grad_in, output = tie(late, grad_in, output)
    late = jnp.sum(late.astype(F32), axis=0).astype(BF)
    late_parts = [late] + [lax.ppermute(late, "zh", shift(o)) for o in OFFSETS[1:]]
    late = sum(part.astype(F32) for part in late_parts).astype(BF)
    late_parts = [late] + [lax.ppermute(late, "x", unshift(o)) for o in OFFSETS[1:]]
    late_parts = placed_at([part.astype(F32) for part in late_parts], x_at)
    lines = lines // 4
    grad_out = jnp.concatenate([part[:lines] for part in late_parts], axis=0)
    late_parts = [part[lines:] for part in late_parts]
    share = w_qkv.shape[0]
    deep = wide * share // width
    part_q = [part[:deep].reshape(share, wide) for part in late_parts]
    part_kv = [part[deep:].reshape(share, 2 * wide) for part in late_parts]
    grad_qkv = jnp.concatenate(
        part_q + [part[:, :wide] for part in part_kv] + [part[:, wide:] for part in part_kv],
        axis=1,
    )
    return (output[None], grad_in[None], grad_qkv, grad_out)


def solution(mesh):
    split = Mesh(mesh.devices.reshape(4, 4, 2, 4, 2), BLK + FSDP)
    placed = (
        P(FSDP, BLK, None),
        P(FSDP, BLK, None),
        P(FSDP, BLK, None),
        P(FSDP, None),
        P(FSDP, None),
        P(),
    )
    return jax.shard_map(
        on_device,
        mesh=split,
        in_specs=placed,
        out_specs=(
            P(FSDP, BLK, None),
            P(FSDP, BLK, None),
            P(FSDP, None),
            P(FSDP, None),
        ),
        check_vma=False,
    )
```
